512 devices in a mesh: section: 32 (over z_lo, x, core), mp: 16 (over z_hi, y).
Axes of the slice: x: 4, y: 8, z: 8 (z_hi: 2, z_lo: 4; z = z_hi * 4 + z_lo), core: 2. Of those that a mesh axis runs over, the one named last changes fastest.
Arguments:
- queries: bfloat16 [32, 2, 64, 4096], P('section', None, None, 'mp'), may hold values from -48 to 48
- memory: bfloat16 [2, 128, 4096], P(None, None, 'section'), may hold values from -6 to 6
- key_weight: bfloat16 [32, 4096, 4096], P('section', None, 'mp'), may hold values from -0.09375 to 0.09375
- value_weight: bfloat16 [32, 4096, 4096], P('section', None, 'mp'), may hold values from -0.09375 to 0.09375
- context_grad: bfloat16 [32, 2, 64, 4096], P('section', None, None, 'mp'), may hold values from -6 to 6
Outputs:
- passed_context: bfloat16 [32, 2, 64, 4096], P('section', None, None, 'mp')
- passed_query_grad: bfloat16 [32, 2, 64, 4096], P('section', None, None, 'mp')
- memory_grad: float32 [2, 128, 4096], P(None, None, 'section')
The draws below stay inside these ranges and needn't reach their ends.
All inputs are finite; a program needn't handle non-finite values.
Results may differ from the reference program's by a relative error of at most 0.012.
The reference program's roundings to bfloat16 on the way (of `key_rows`, `value_rows`, `prob_low`, `context`, `grad_scores` and `query_grad`) count: a program that leaves them out, or rounds other values in their place, can miss the bound.
Values may be sent and summed in bfloat16 or wider, within the bound.
No kernel may reach another device: no remote copies, remote signals or barrier semaphores. Data moves between devices by JAX's collectives and lax.ppermute only.
A program may use at most 64 MiB of HBM per device.

```python
import jax
import jax.numpy as jnp
from jax import lax

D = 4096
HEADS = 16
HEAD_DIM = 256
MICRO = 2
DEC = 64
MEM = 128
LAYERS = 32
HH = 4096


def draw_queries(key, part):
    key = jax.random.fold_in(key, 11)
    first_key = jax.random.fold_in(key, 0)
    base = jax.random.normal(first_key, (LAYERS, MICRO, DEC, HEADS * HEAD_DIM), jnp.float32)
    return jnp.clip(base, -6.0, 6.0).astype(jnp.bfloat16)


def level_of(rng, extent, shards, least, top_value):
    gain = 1.0
    for axis_at, parts in shards:
        steps = jax.random.uniform(jax.random.fold_in(jax.random.fold_in(rng, 6), axis_at), (parts,), jnp.float32, least / len(shards), top_value / len(shards))
        gain = gain * jnp.repeat(jnp.exp(steps), extent[axis_at] // parts).reshape((-1,) + (1,) * (len(extent) - 1 - axis_at))
    return gain


def scatter_about(rng, extent, scale, bound, shards=(), held_as=jnp.bfloat16):
    drawn = scale * jax.random.normal(rng, extent, jnp.float32)
    if shards:
        drawn = drawn * level_of(rng, extent, shards, -0.22, 0.18)
    return jnp.clip(drawn, -bound, bound).astype(held_as)


def setup_inputs(seed: int = 0) -> dict:
    key_list = jax.random.split(jax.random.key(seed), 6)
    return {
        "queries": draw_queries(jax.random.fold_in(key_list[5], 71), 0),
        "memory": scatter_about(key_list[1], (MICRO, MEM, D), 1.0, 6.0, ((2, 32),)),
        "key_weight": scatter_about(key_list[2], (LAYERS, D, HH), D ** -0.5, 0.09375, ((0, 32), (2, 16))),
        "value_weight": scatter_about(key_list[3], (LAYERS, D, HH), D ** -0.5, 0.09375, ((0, 32), (2, 16))),
        "context_grad": scatter_about(key_list[4], (LAYERS, MICRO, DEC, HH), 1.0, 6.0, ((0, 32), (3, 16))),
    }


def attend(query_heads, key_heads, value_heads, grad_heads):
    scale = HEAD_DIM ** -0.5
    query_float = query_heads.astype(jnp.float32)
    key_float = key_heads.astype(jnp.float32)
    value_float = value_heads.astype(jnp.float32)
    grad_float = grad_heads.astype(jnp.float32)
    scores = jnp.einsum("bqhd,bkhd->bhqk", query_float, key_float) * scale
    attention = jax.nn.softmax(scores, axis=-1)
    prob_low = lax.optimization_barrier(attention.astype(jnp.bfloat16))
    prob_float = prob_low.astype(jnp.float32)
    context = jnp.einsum("bhqk,bkhd->bqhd", prob_float, value_float).astype(jnp.bfloat16)
    grad_probs = jnp.einsum("bqhd,bkhd->bhqk", grad_float, value_float)
    row_dot = jnp.sum(attention * grad_probs, axis=-1, keepdims=True)
    grad_scores = lax.optimization_barrier((attention * (grad_probs - row_dot) * scale).astype(jnp.bfloat16))
    grad_float_scores = grad_scores.astype(jnp.float32)
    query_grad = jnp.einsum("bhqk,bkhd->bqhd", grad_float_scores, key_float).astype(jnp.bfloat16)
    key_grad = jnp.einsum("bhqk,bqhd->bkhd", grad_float_scores, query_float).astype(jnp.bfloat16)
    value_grad = jnp.einsum("bhqk,bqhd->bkhd", prob_float, grad_float).astype(jnp.bfloat16)
    return context, query_grad, key_grad, value_grad


def reference(queries, memory, key_weight, value_weight, context_grad):
    flat_memory = memory.reshape(MICRO * MEM, D)

    def layer(total, inputs):
        query_layer, key_layer, value_layer, grad_layer = inputs
        key_rows = jnp.dot(flat_memory, key_layer, preferred_element_type=jnp.float32).astype(jnp.bfloat16)
        value_rows = jnp.dot(flat_memory, value_layer, preferred_element_type=jnp.float32).astype(jnp.bfloat16)
        context, query_grad, key_grad, value_grad = attend(
            query_layer.reshape(MICRO, DEC, HEADS, HEAD_DIM),
            key_rows.reshape(MICRO, MEM, HEADS, HEAD_DIM),
            value_rows.reshape(MICRO, MEM, HEADS, HEAD_DIM),
            grad_layer.reshape(MICRO, DEC, HEADS, HEAD_DIM))
        contribution = jnp.dot(key_grad.reshape(MICRO * MEM, HH), key_layer.T, preferred_element_type=jnp.float32)
        contribution = contribution + jnp.dot(value_grad.reshape(MICRO * MEM, HH), value_layer.T, preferred_element_type=jnp.float32)
        return total + contribution, (context.reshape(MICRO, DEC, HH), query_grad.reshape(MICRO, DEC, HH))

    total, (contexts, query_grads) = lax.scan(
        layer, jnp.zeros((MICRO * MEM, D), jnp.float32), (queries, key_weight, value_weight, context_grad))
    passed_context = jnp.concatenate([jnp.zeros_like(contexts[:1]), contexts[:-1]], axis=0)
    passed_query_grad = jnp.concatenate([query_grads[1:], jnp.zeros_like(query_grads[:1])], axis=0)
    return passed_context, passed_query_grad, total.reshape(MICRO, MEM, D)
```

```python
import jax
import jax.numpy as jnp
from jax import lax
from jax.sharding import Mesh, PartitionSpec as P

HEAD_DIM = 256
AXES = ("z_lo", "x", "core", "z_hi", "y")
SIZES = (4, 4, 2, 2, 8)
CHIPS = 16
PART = 128


def index_of(z_lo, x, core, z_hi, y):
    return (((z_lo * 4 + x) * 2 + core) * 2 + z_hi) * 8 + y


def routes(step):
    pairs = []
    for chip in range(CHIPS):
        for core in range(2):
            to = step(chip, core)
            if to is None:
                continue
            for z_hi in range(2):
                for y in range(8):
                    pairs.append((
                        index_of(chip // 4, chip % 4, core, z_hi, y),
                        index_of(to[0] // 4, to[0] % 4, to[1], z_hi, y),
                    ))
    return pairs


def to_sibling(block):
    return lax.ppermute(block, AXES, routes(lambda chip, core: (chip, 1 - core)))


def to_next_chip(block):
    def step(chip, core):
        chip = chip + 1 if core == 1 else chip - 1
        return (chip, 1 - core) if 0 <= chip < CHIPS else None

    return lax.ppermute(block, AXES, routes(step))


def attend_local(query_heads, key_heads, value_heads, grad_heads):
    scale = HEAD_DIM ** (-0.5)
    scores = (
        jnp.einsum("bqd,bkd->bqk", query_heads, key_heads, preferred_element_type=jnp.float32)
        * scale
    )
    attention = jax.nn.softmax(scores, axis=-1)
    prob_low = attention.astype(jnp.bfloat16)
    context = jnp.einsum(
        "bqk,bkd->bqd", prob_low, value_heads, preferred_element_type=jnp.float32
    ).astype(jnp.bfloat16)
    grad_probs = jnp.einsum(
        "bqd,bkd->bqk", grad_heads, value_heads, preferred_element_type=jnp.float32
    )
    row_dot = jnp.sum(attention * grad_probs, axis=-1, keepdims=True)
    grad_scores = (attention * (grad_probs - row_dot) * scale).astype(jnp.bfloat16)
    query_grad = jnp.einsum(
        "bqk,bkd->bqd", grad_scores, key_heads, preferred_element_type=jnp.float32
    ).astype(jnp.bfloat16)
    key_grad = jnp.einsum(
        "bqk,bqd->bkd", grad_scores, query_heads, preferred_element_type=jnp.float32
    ).astype(jnp.bfloat16)
    value_grad = jnp.einsum(
        "bqk,bqd->bkd", prob_low, grad_heads, preferred_element_type=jnp.float32
    ).astype(jnp.bfloat16)
    return (context, query_grad, key_grad, value_grad)


def per_device(queries, memory, key_weight, value_weight, context_grad):
    core = lax.axis_index("core")
    key_layer = key_weight[0]
    value_layer = value_weight[0]
    own = memory.reshape(1, 256, PART)
    mine = lax.all_to_all(
        jnp.broadcast_to(own, (CHIPS, 256, PART)), ("z_lo", "x"), 0, 0, tiled=True
    )
    other = to_sibling(mine)
    first = jnp.where(core == 0, mine, other)
    second = jnp.where(core == 0, other, mine)
    portion = jnp.stack([first, second], axis=1)
    portion = portion.transpose(2, 0, 1, 3).reshape(256, 4096)
    key_rows = jnp.dot(portion, key_layer, preferred_element_type=jnp.float32)
    value_rows = jnp.dot(portion, value_layer, preferred_element_type=jnp.float32)
    key_rows = key_rows.astype(jnp.bfloat16).reshape(2, 128, 256)
    value_rows = value_rows.astype(jnp.bfloat16).reshape(2, 128, 256)
    context, query_grad, key_grad, value_grad = attend_local(
        queries[0], key_rows, value_rows, context_grad[0]
    )
    contribution = jnp.dot(
        key_grad.reshape(256, 256), key_layer.T, preferred_element_type=jnp.float32
    )
    contribution = contribution + jnp.dot(
        value_grad.reshape(256, 256), value_layer.T, preferred_element_type=jnp.float32
    )
    split = contribution.reshape(256, CHIPS, 2, PART)
    keep = lax.dynamic_index_in_dim(split, core, 2, keepdims=False).transpose(1, 0, 2)
    give = lax.dynamic_index_in_dim(split, 1 - core, 2, keepdims=False).transpose(1, 0, 2)
    inside = jnp.where(core == 0, context, query_grad).reshape(1, 256, PART)
    across = jnp.where(core == 0, query_grad, context)
    swapped = to_sibling(jnp.concatenate([give.astype(jnp.bfloat16), inside], axis=0))
    got_across = to_next_chip(across)
    got_inside = swapped[CHIPS].reshape(2, 64, 256)
    passed_context = jnp.where(core == 0, got_across, got_inside)
    passed_query_grad = jnp.where(core == 0, got_inside, got_across)
    chip_sum = (keep + swapped[:CHIPS].astype(jnp.float32)).astype(jnp.bfloat16)
    pieces = lax.all_to_all(
        chip_sum.reshape(CHIPS * 8, 32, PART), ("z_lo", "x", "y"), 0, 0, tiled=True
    )
    piece = jnp.sum(pieces.astype(jnp.float32), axis=0).astype(jnp.bfloat16)
    whole = lax.all_to_all(
        jnp.broadcast_to(piece[None], (16, 32, PART)), ("z_hi", "y"), 0, 0, tiled=True
    )
    halves = whole.reshape(2, 256, PART).astype(jnp.float32)
    memory_grad = (halves[0] + halves[1]).reshape(2, 128, PART)
    return (passed_context[None], passed_query_grad[None], memory_grad)


def solution(mesh):
    fine = Mesh(mesh.devices.reshape(SIZES), AXES)
    section = ("z_lo", "x", "core")
    mp = ("z_hi", "y")
    in_specs = (
        P(section, None, None, mp),
        P(None, None, section),
        P(section, None, mp),
        P(section, None, mp),
        P(section, None, None, mp),
    )
    out_specs = (
        P(section, None, None, mp),
        P(section, None, None, mp),
        P(None, None, section),
    )
    return jax.shard_map(
        per_device, mesh=fine, in_specs=in_specs, out_specs=out_specs, check_vma=False
    )
```

```python
import jax
import jax.numpy as jnp
from jax import lax
from jax.experimental import pallas as pl
from jax.experimental.pallas import tpu as pltpu
from jax.sharding import Mesh, PartitionSpec as P

HEAD_DIM = 256
AXES = ("z_lo", "x", "core", "z_hi", "y")
SIZES = (4, 4, 2, 2, 8)
CHIPS = 16
PART = 128


def index_of(z_lo, x, core, z_hi, y):
    return (((z_lo * 4 + x) * 2 + core) * 2 + z_hi) * 8 + y


def routes(step):
    pairs = []
    for chip in range(CHIPS):
        for core in range(2):
            to = step(chip, core)
            if to is None:
                continue
            for z_hi in range(2):
                for y in range(8):
                    pairs.append((
                        index_of(chip // 4, chip % 4, core, z_hi, y),
                        index_of(to[0] // 4, to[0] % 4, to[1], z_hi, y),
                    ))
    return pairs


def to_sibling(block):
    return lax.ppermute(block, AXES, routes(lambda chip, core: (chip, 1 - core)))


def to_next_chip(block):
    def step(chip, core):
        chip = chip + 1 if core == 1 else chip - 1
        return (chip, 1 - core) if 0 <= chip < CHIPS else None

    return lax.ppermute(block, AXES, routes(step))


def pair(ref, block, parity):
    low = ref[pl.ds(pl.multiple_of((4 * block + parity) * PART, PART), PART), :]
    high = ref[pl.ds(pl.multiple_of((4 * block + 2 + parity) * PART, PART), PART), :]
    return jnp.concatenate([low, high], axis=0)


def dot(a, b, contract):
    return lax.dot_general(a, b, (contract, ((), ())), preferred_element_type=jnp.float32)


def partial_rows(features, key_ref, value_ref, parity, key_sum, value_sum):
    for block in range(CHIPS // 2):
        tile = jnp.concatenate([features[2 * block], features[2 * block + 1]], axis=1)
        key_part = dot(tile, pair(key_ref, block, parity), ((1,), (0,)))
        value_part = dot(tile, pair(value_ref, block, parity), ((1,), (0,)))
        key_sum = key_part if key_sum is None else key_sum + key_part
        value_sum = value_part if value_sum is None else value_sum + value_part
    return key_sum, value_sum


def contribute(key_grad, value_grad, key_ref, value_ref, parity, block):
    part = dot(key_grad, pair(key_ref, block, parity), ((1,), (1,)))
    return part + dot(value_grad, pair(value_ref, block, parity), ((1,), (1,)))


def begin_kernel(core_ref, mine_ref, key_ref, value_ref, sum_ref):
    key_sum, value_sum = partial_rows(mine_ref, key_ref, value_ref, core_ref[0], None, None)
    sum_ref[0] = key_sum
    sum_ref[1] = value_sum


def attend_kernel(
    core_ref, other_ref, sum_ref, key_ref, value_ref, query_ref, grad_ref,
    give_ref, across_ref, grads_ref,
):
    core = core_ref[0]
    scale = HEAD_DIM ** (-0.5)
    key_sum, value_sum = partial_rows(
        other_ref, key_ref, value_ref, 1 - core, sum_ref[0], sum_ref[1]
    )
    key_rows = key_sum.astype(jnp.bfloat16)
    value_rows = value_sum.astype(jnp.bfloat16)
    contexts, query_grads = [], []
    for micro in range(2):
        keys = key_rows[micro * 128:(micro + 1) * 128]
        values = value_rows[micro * 128:(micro + 1) * 128]
        query = query_ref[micro]
        grad = grad_ref[micro]
        scores = dot(query, keys, ((1,), (1,))) * scale
        grad_probs = dot(grad, values, ((1,), (1,)))
        raised = jnp.exp(scores - jnp.max(scores, axis=-1, keepdims=True))
        attention = raised / jnp.sum(raised, axis=-1, keepdims=True)
        prob_low = attention.astype(jnp.bfloat16)
        row_dot = jnp.sum(attention * grad_probs, axis=-1, keepdims=True)
        grad_scores = (attention * (grad_probs - row_dot) * scale).astype(jnp.bfloat16)
        contexts.append(dot(prob_low, values, ((1,), (0,))).astype(jnp.bfloat16))
        query_grads.append(dot(grad_scores, keys, ((1,), (0,))).astype(jnp.bfloat16))
        rows = slice(micro * 128, (micro + 1) * 128)
        grads_ref[0, rows] = dot(grad_scores, query, ((0,), (0,))).astype(jnp.bfloat16)
        grads_ref[1, rows] = dot(prob_low, grad, ((0,), (0,))).astype(jnp.bfloat16)
    context = jnp.concatenate(contexts, axis=0)
    query_grad = jnp.concatenate(query_grads, axis=0)
    inside = jnp.where(core == 0, context, query_grad)
    across_ref[...] = jnp.where(core == 0, query_grad, context)
    give_ref[CHIPS, :128] = inside[:, :PART]
    give_ref[CHIPS, 128:] = inside[:, PART:]
    for block in range(CHIPS // 2):
        part = contribute(grads_ref[0], grads_ref[1], key_ref, value_ref, 1 - core, block)
        part = part.astype(jnp.bfloat16)
        give_ref[2 * block] = part[:, :PART]
        give_ref[2 * block + 1] = part[:, PART:]


def finish_kernel(core_ref, grads_ref, swapped_ref, key_ref, value_ref, total_ref):
    core = core_ref[0]
    for block in range(CHIPS // 2):
        part = contribute(grads_ref[0], grads_ref[1], key_ref, value_ref, core, block)
        low = part[:, :PART] + swapped_ref[2 * block].astype(jnp.float32)
        high = part[:, PART:] + swapped_ref[2 * block + 1].astype(jnp.float32)
        total_ref[2 * block] = low.astype(jnp.bfloat16)
        total_ref[2 * block + 1] = high.astype(jnp.bfloat16)


def call(kernel, outs, flops, *args):
    specs = [pl.BlockSpec(memory_space=pltpu.SMEM)]
    specs += [pl.BlockSpec(memory_space=pltpu.VMEM)] * (len(args) - 1)
    return pl.pallas_call(
        kernel,
        out_shape=outs,
        in_specs=specs,
        out_specs=[pl.BlockSpec(memory_space=pltpu.VMEM)] * len(outs),
        compiler_params=pltpu.CompilerParams(vmem_limit_bytes=32 * 2**20),
        cost_estimate=pl.CostEstimate(flops=flops, bytes_accessed=2**22, transcendentals=0),
    )(*args)


def per_device(queries, memory, key_weight, value_weight, context_grad):
    core = lax.axis_index("core")
    core_at = core.astype(jnp.int32).reshape(1)
    key_layer = key_weight[0]
    value_layer = value_weight[0]
    low, full = jnp.bfloat16, jnp.float32
    own = memory.reshape(1, 256, PART)
    mine = lax.all_to_all(
        jnp.broadcast_to(own, (CHIPS, 256, PART)), ("z_lo", "x"), 0, 0, tiled=True
    )
    other = to_sibling(mine)
    (sums,) = call(
        begin_kernel, [jax.ShapeDtypeStruct((2, 256, 256), full)], 2**29,
        core_at, mine, key_layer, value_layer,
    )
    give, across, grads = call(
        attend_kernel,
        [
            jax.ShapeDtypeStruct((CHIPS + 1, 256, PART), low),
            jax.ShapeDtypeStruct((128, 256), low),
            jax.ShapeDtypeStruct((2, 256, 256), low),
        ],
        2**30,
        core_at, other, sums, key_layer, value_layer, queries[0], context_grad[0],
    )
    swapped = to_sibling(give)
    got_across = to_next_chip(across)
    (chip_sum,) = call(
        finish_kernel, [jax.ShapeDtypeStruct((CHIPS, 256, PART), low)], 2**29,
        core_at, grads, swapped, key_layer, value_layer,
    )
    pieces = lax.all_to_all(
        chip_sum.reshape(CHIPS * 8, 32, PART), ("z_lo", "x", "y"), 0, 0, tiled=True
    )
    inside = swapped[CHIPS].reshape(2, 2, 64, PART)
    got_inside = jnp.concatenate([inside[0], inside[1]], axis=-1)
    got_across = got_across.reshape(2, 64, 256)
    passed_context = jnp.where(core == 0, got_across, got_inside)
    passed_query_grad = jnp.where(core == 0, got_inside, got_across)
    piece = jnp.sum(pieces.astype(full), axis=0).astype(low)
    whole = lax.all_to_all(
        jnp.broadcast_to(piece[None], (16, 32, PART)), ("z_hi", "y"), 0, 0, tiled=True
    )
    halves = whole.reshape(2, 256, PART).astype(full)
    memory_grad = (halves[0] + halves[1]).reshape(2, 128, PART)
    return (passed_context[None], passed_query_grad[None], memory_grad)


def solution(mesh):
    fine = Mesh(mesh.devices.reshape(SIZES), AXES)
    section = ("z_lo", "x", "core")
    mp = ("z_hi", "y")
    in_specs = (
        P(section, None, None, mp),
        P(None, None, section),
        P(section, None, mp),
        P(section, None, mp),
        P(section, None, None, mp),
    )
    out_specs = (
        P(section, None, None, mp),
        P(section, None, None, mp),
        P(None, None, section),
    )
    return jax.shard_map(
        per_device, mesh=fine, in_specs=in_specs, out_specs=out_specs, check_vma=False
    )
```

```python
import jax
import jax.numpy as jnp
from jax import lax
from jax.experimental import pallas as pl
from jax.experimental.pallas import tpu as pltpu
from jax.sharding import Mesh, PartitionSpec as P

HEAD_DIM = 256
AXES = ("z_lo", "x", "core", "z_hi", "y")
SIZES = (4, 4, 2, 2, 8)
CHIPS = 16
PART = 128


def index_of(z_lo, x, core, z_hi, y):
    return (((z_lo * 4 + x) * 2 + core) * 2 + z_hi) * 8 + y


def routes(step):
    pairs = []
    for chip in range(CHIPS):
        for core in range(2):
            to = step(chip, core)
            if to is None:
                continue
            for z_hi in range(2):
                for y in range(8):
                    pairs.append((
                        index_of(chip // 4, chip % 4, core, z_hi, y),
                        index_of(to[0] // 4, to[0] % 4, to[1], z_hi, y),
                    ))
    return pairs


def to_sibling(block):
    return lax.ppermute(block, AXES, routes(lambda chip, core: (chip, 1 - core)))


def to_next_chip(block):
    def step(chip, core):
        chip = chip + 1 if core == 1 else chip - 1
        return (chip, 1 - core) if 0 <= chip < CHIPS else None

    return lax.ppermute(block, AXES, routes(step))


def place(chip):
    return chip % 4 * 4 + chip // 4


def pair(ref, block, parity):
    low = ref[pl.ds(pl.multiple_of((4 * block + parity) * PART, PART), PART), :]
    high = ref[pl.ds(pl.multiple_of((4 * block + 2 + parity) * PART, PART), PART), :]
    return jnp.concatenate([low, high], axis=0)


def dot(a, b, contract):
    return lax.dot_general(a, b, (contract, ((), ())), preferred_element_type=jnp.float32)


def block_of(features, chip):
    z_lo, x = chip // 4, chip % 4
    return jnp.concatenate([features[x, z_lo], features[x, 4 + z_lo]], axis=0)


def partial_rows(features, key_ref, value_ref, parity, key_sum, value_sum):
    for block in range(CHIPS // 2):
        sides = [block_of(features, 2 * block), block_of(features, 2 * block + 1)]
        tile = jnp.concatenate(sides, axis=1)
        key_part = dot(tile, pair(key_ref, block, parity), ((1,), (0,)))
        value_part = dot(tile, pair(value_ref, block, parity), ((1,), (0,)))
        key_sum = key_part if key_sum is None else key_sum + key_part
        value_sum = value_part if value_sum is None else value_sum + value_part
    return key_sum, value_sum


def contribute(key_grad, value_grad, key_ref, value_ref, parity, block):
    part = dot(key_grad, pair(key_ref, block, parity), ((1,), (1,)))
    return part + dot(value_grad, pair(value_ref, block, parity), ((1,), (1,)))


def begin_kernel(core_ref, mine_ref, key_ref, value_ref, sum_ref):
    key_sum, value_sum = partial_rows(mine_ref, key_ref, value_ref, core_ref[0], None, None)
    sum_ref[0] = key_sum
    sum_ref[1] = value_sum


def attend_kernel(
    core_ref, other_ref, sum_ref, key_ref, value_ref, query_ref, grad_ref,
    give_ref, across_ref, grads_ref,
):
    core = core_ref[0]
    scale = HEAD_DIM ** (-0.5)
    key_sum, value_sum = partial_rows(
        other_ref, key_ref, value_ref, 1 - core, sum_ref[0], sum_ref[1]
    )
    key_rows = key_sum.astype(jnp.bfloat16)
    value_rows = value_sum.astype(jnp.bfloat16)
    contexts, query_grads = [], []
    for micro in range(2):
        keys = key_rows[micro * 128:(micro + 1) * 128]
        values = value_rows[micro * 128:(micro + 1) * 128]
        query = query_ref[micro]
        grad = grad_ref[micro]
        scores = dot(query, keys, ((1,), (1,))) * scale
        grad_probs = dot(grad, values, ((1,), (1,)))
        raised = jnp.exp(scores - jnp.max(scores, axis=-1, keepdims=True))
        attention = raised / jnp.sum(raised, axis=-1, keepdims=True)
        prob_low = attention.astype(jnp.bfloat16)
        row_dot = jnp.sum(attention * grad_probs, axis=-1, keepdims=True)
        grad_scores = (attention * (grad_probs - row_dot) * scale).astype(jnp.bfloat16)
        contexts.append(dot(prob_low, values, ((1,), (0,))).astype(jnp.bfloat16))
        query_grads.append(dot(grad_scores, keys, ((1,), (0,))).astype(jnp.bfloat16))
        rows = slice(micro * 128, (micro + 1) * 128)
        grads_ref[0, rows] = dot(grad_scores, query, ((0,), (0,))).astype(jnp.bfloat16)
        grads_ref[1, rows] = dot(prob_low, grad, ((0,), (0,))).astype(jnp.bfloat16)
    context = jnp.concatenate(contexts, axis=0)
    query_grad = jnp.concatenate(query_grads, axis=0)
    inside = jnp.where(core == 0, context, query_grad)
    across_ref[...] = jnp.where(core == 0, query_grad, context)
    give_ref[CHIPS, :128] = inside[:, :PART]
    give_ref[CHIPS, 128:] = inside[:, PART:]
    for block in range(CHIPS // 2):
        part = contribute(grads_ref[0], grads_ref[1], key_ref, value_ref, 1 - core, block)
        part = part.astype(jnp.bfloat16)
        give_ref[place(2 * block)] = part[:, :PART]
        give_ref[place(2 * block + 1)] = part[:, PART:]


def keep_kernel(core_ref, grads_ref, key_ref, value_ref, keep_ref):
    for block in range(CHIPS // 2):
        part = contribute(grads_ref[0], grads_ref[1], key_ref, value_ref, core_ref[0], block)
        keep_ref[place(2 * block)] = part[:, :PART]
        keep_ref[place(2 * block + 1)] = part[:, PART:]


def add_kernel(core_ref, keep_ref, swapped_ref, total_ref):
    for chip in range(CHIPS):
        total_ref[chip] = (
            keep_ref[chip] + swapped_ref[chip].astype(jnp.float32)
        ).astype(jnp.bfloat16)


def call(kernel, outs, flops, *args):
    specs = [pl.BlockSpec(memory_space=pltpu.SMEM)]
    specs += [pl.BlockSpec(memory_space=pltpu.VMEM)] * (len(args) - 1)
    return pl.pallas_call(
        kernel,
        out_shape=outs,
        in_specs=specs,
        out_specs=[pl.BlockSpec(memory_space=pltpu.VMEM)] * len(outs),
        compiler_params=pltpu.CompilerParams(vmem_limit_bytes=32 * 2**20),
        cost_estimate=pl.CostEstimate(flops=flops, bytes_accessed=2**22, transcendentals=0),
    )(*args)


def per_device(queries, memory, key_weight, value_weight, context_grad):
    core = lax.axis_index("core")
    core_at = core.astype(jnp.int32).reshape(1)
    key_layer, value_layer = key_weight[0], value_weight[0]
    low, full = jnp.bfloat16, jnp.float32
    half = lax.dynamic_slice_in_dim(memory, lax.axis_index("z_hi"), 1, 0)
    column = lax.all_to_all(
        jnp.broadcast_to(half, (8, 128, PART)), ("z_hi", "z_lo"), 0, 0, tiled=True
    )
    mine = lax.all_to_all(
        jnp.broadcast_to(column.reshape(1, 8, 128, PART), (4, 8, 128, PART)), "x", 0, 0, tiled=True
    )
    other = to_sibling(mine)
    (sums,) = call(
        begin_kernel, [jax.ShapeDtypeStruct((2, 256, 256), full)], 2**29,
        core_at, mine, key_layer, value_layer,
    )
    give, across, grads = call(
        attend_kernel,
        [
            jax.ShapeDtypeStruct((CHIPS + 1, 256, PART), low),
            jax.ShapeDtypeStruct((128, 256), low),
            jax.ShapeDtypeStruct((2, 256, 256), low),
        ],
        2**30,
        core_at, other, sums, key_layer, value_layer, queries[0], context_grad[0],
    )
    swapped = to_sibling(give)
    got_across = to_next_chip(across)
    (keep,) = call(
        keep_kernel, [jax.ShapeDtypeStruct((CHIPS, 256, PART), full)], 2**30,
        core_at, grads, key_layer, value_layer,
    )
    (chip_sum,) = call(
        add_kernel, [jax.ShapeDtypeStruct((CHIPS, 256, PART), low)], 2**20,
        core_at, keep, swapped,
    )
    rows = lax.all_to_all(chip_sum.reshape(4, 4 * 256, PART), "x", 0, 0, tiled=True)
    row_sum = jnp.sum(rows.astype(full), axis=0).astype(low)
    pieces = lax.all_to_all(row_sum.reshape(32, 32, PART), ("z_lo", "y"), 0, 0, tiled=True)
    inside = swapped[CHIPS].reshape(2, 2, 64, PART)
    got_inside = jnp.concatenate([inside[0], inside[1]], axis=-1)
    got_across = got_across.reshape(2, 64, 256)
    passed_context = jnp.where(core == 0, got_across, got_inside)
    passed_query_grad = jnp.where(core == 0, got_inside, got_across)
    pieces, passed_context, passed_query_grad = lax.optimization_barrier(
        (pieces, passed_context, passed_query_grad)
    )
    piece = jnp.sum(pieces.astype(full), axis=0).astype(low)
    whole = lax.all_to_all(
        jnp.broadcast_to(piece[None], (16, 32, PART)), ("z_hi", "y"), 0, 0, tiled=True
    )
    halves = whole.reshape(2, 256, PART).astype(full)
    memory_grad = (halves[0] + halves[1]).reshape(2, 128, PART)
    return (passed_context[None], passed_query_grad[None], memory_grad)


def solution(mesh):
    fine = Mesh(mesh.devices.reshape(SIZES), AXES)
    section = ("z_lo", "x", "core")
    mp = ("z_hi", "y")
    in_specs = (
        P(section, None, None, mp),
        P(None, None, section),
        P(section, None, mp),
        P(section, None, mp),
        P(section, None, None, mp),
    )
    out_specs = (
        P(section, None, None, mp),
        P(section, None, None, mp),
        P(None, None, section),
    )
    return jax.shard_map(
        per_device, mesh=fine, in_specs=in_specs, out_specs=out_specs, check_vma=False
    )
```

```python
import jax
import jax.numpy as jnp
from jax import lax
from jax.experimental import pallas as pl
from jax.experimental.pallas import tpu as pltpu
from jax.sharding import Mesh, PartitionSpec as P

HEAD_DIM = 256
AXES = ("zq", "zb", "x", "core", "z_hi", "yq", "yb")
SIZES = (2, 2, 4, 2, 2, 4, 2)
CHIPS = 16
PART = 128


def index_of(z_lo, x, core, z_hi, y):
    return (((z_lo * 4 + x) * 2 + core) * 2 + z_hi) * 8 + y


def routes(step):
    pairs = []
    for chip in range(CHIPS):
        for core in range(2):
            to = step(chip, core)
            if to is None:
                continue
            for z_hi in range(2):
                for y in range(8):
                    pairs.append((
                        index_of(chip // 4, chip % 4, core, z_hi, y),
                        index_of(to[0] // 4, to[0] % 4, to[1], z_hi, y),
                    ))
    return pairs


def to_sibling(block):
    return lax.ppermute(block, AXES, routes(lambda chip, core: (chip, 1 - core)))


def to_next_chip(block):
    def step(chip, core):
        chip = chip + 1 if core == 1 else chip - 1
        return (chip, 1 - core) if 0 <= chip < CHIPS else None

    return lax.ppermute(block, AXES, routes(step))


def pair(ref, block, parity):
    low = ref[pl.ds(pl.multiple_of((4 * block + parity) * PART, PART), PART), :]
    high = ref[pl.ds(pl.multiple_of((4 * block + 2 + parity) * PART, PART), PART), :]
    return jnp.concatenate([low, high], axis=0)


def dot(a, b, contract):
    return lax.dot_general(a, b, (contract, ((), ())), preferred_element_type=jnp.float32)


def block_of(features, chip):
    z_lo, x = chip // 4, chip % 4
    zb, zq = z_lo % 2, z_lo // 2
    return jnp.concatenate([features[x, 0, zb, zq], features[x, 1, zb, zq]], axis=0)


def partial_rows(features, key_ref, value_ref, parity, key_sum, value_sum):
    for block in range(CHIPS // 2):
        sides = [block_of(features, 2 * block), block_of(features, 2 * block + 1)]
        tile = jnp.concatenate(sides, axis=1)
        key_part = dot(tile, pair(key_ref, block, parity), ((1,), (0,)))
        value_part = dot(tile, pair(value_ref, block, parity), ((1,), (0,)))
        key_sum = key_part if key_sum is None else key_sum + key_part
        value_sum = value_part if value_sum is None else value_sum + value_part
    return key_sum, value_sum


def contribute(key_grad, value_grad, key_ref, value_ref, parity, block):
    part = dot(key_grad, pair(key_ref, block, parity), ((1,), (1,)))
    return part + dot(value_grad, pair(value_ref, block, parity), ((1,), (1,)))


def begin_kernel(core_ref, mine_ref, key_ref, value_ref, sum_ref):
    key_sum, value_sum = partial_rows(mine_ref, key_ref, value_ref, core_ref[0], None, None)
    sum_ref[0] = key_sum
    sum_ref[1] = value_sum


def attend_kernel(
    core_ref, other_ref, sum_ref, key_ref, value_ref, query_ref, grad_ref,
    give_ref, across_ref, grads_ref,
):
    core = core_ref[0]
    scale = HEAD_DIM ** (-0.5)
    key_sum, value_sum = partial_rows(
        other_ref, key_ref, value_ref, 1 - core, sum_ref[0], sum_ref[1]
    )
    key_rows = key_sum.astype(jnp.bfloat16)
    value_rows = value_sum.astype(jnp.bfloat16)
    contexts, query_grads = [], []
    for micro in range(2):
        keys = key_rows[micro * 128:(micro + 1) * 128]
        values = value_rows[micro * 128:(micro + 1) * 128]
        query = query_ref[micro]
        grad = grad_ref[micro]
        scores = dot(query, keys, ((1,), (1,))) * scale
        grad_probs = dot(grad, values, ((1,), (1,)))
        raised = jnp.exp(scores - jnp.max(scores, axis=-1, keepdims=True))
        attention = raised / jnp.sum(raised, axis=-1, keepdims=True)
        prob_low = attention.astype(jnp.bfloat16)
        row_dot = jnp.sum(attention * grad_probs, axis=-1, keepdims=True)
        grad_scores = (attention * (grad_probs - row_dot) * scale).astype(jnp.bfloat16)
        contexts.append(dot(prob_low, values, ((1,), (0,))).astype(jnp.bfloat16))
        query_grads.append(dot(grad_scores, keys, ((1,), (0,))).astype(jnp.bfloat16))
        rows = slice(micro * 128, (micro + 1) * 128)
        grads_ref[0, rows] = dot(grad_scores, query, ((0,), (0,))).astype(jnp.bfloat16)
        grads_ref[1, rows] = dot(prob_low, grad, ((0,), (0,))).astype(jnp.bfloat16)
    context = jnp.concatenate(contexts, axis=0)
    query_grad = jnp.concatenate(query_grads, axis=0)
    inside = jnp.where(core == 0, context, query_grad)
    across_ref[...] = jnp.where(core == 0, query_grad, context)
    give_ref[CHIPS, :128] = inside[:, :PART]
    give_ref[CHIPS, 128:] = inside[:, PART:]
    for block in range(CHIPS // 2):
        part = contribute(grads_ref[0], grads_ref[1], key_ref, value_ref, 1 - core, block)
        part = part.astype(jnp.bfloat16)
        give_ref[2 * block] = part[:, :PART]
        give_ref[2 * block + 1] = part[:, PART:]


def keep_kernel(core_ref, grads_ref, key_ref, value_ref, keep_ref):
    for block in range(CHIPS // 2):
        part = contribute(grads_ref[0], grads_ref[1], key_ref, value_ref, core_ref[0], block)
        keep_ref[2 * block] = part[:, :PART]
        keep_ref[2 * block + 1] = part[:, PART:]


def add_kernel(core_ref, keep_ref, swapped_ref, total_ref):
    for chip in range(CHIPS):
        z_lo, x = chip // 4, chip % 4
        total = keep_ref[chip] + swapped_ref[chip].astype(jnp.float32)
        total = total.astype(jnp.bfloat16)
        total_ref[x, 0, z_lo % 2, z_lo // 2] = total[:128]
        total_ref[x, 1, z_lo % 2, z_lo // 2] = total[128:]


def call(kernel, outs, flops, *args):
    specs = [pl.BlockSpec(memory_space=pltpu.SMEM)]
    specs += [pl.BlockSpec(memory_space=pltpu.VMEM)] * (len(args) - 1)
    return pl.pallas_call(
        kernel,
        out_shape=outs,
        in_specs=specs,
        out_specs=[pl.BlockSpec(memory_space=pltpu.VMEM)] * len(outs),
        compiler_params=pltpu.CompilerParams(vmem_limit_bytes=32 * 2**20),
        cost_estimate=pl.CostEstimate(flops=flops, bytes_accessed=2**22, transcendentals=0),
    )(*args)


def per_device(queries, memory, key_weight, value_weight, context_grad):
    core = lax.axis_index("core")
    core_at = core.astype(jnp.int32).reshape(1)
    key_layer, value_layer = key_weight[0], value_weight[0]
    low, full = jnp.bfloat16, jnp.float32
    half = lax.dynamic_slice_in_dim(memory, lax.axis_index("yb"), 1, 0)
    column = lax.all_to_all(jnp.broadcast_to(half, (2, 128, PART)), "zq", 0, 0, tiled=True)
    mine = lax.all_to_all(
        jnp.broadcast_to(column.reshape(1, 256, PART), (16, 256, PART)),
        ("x", "yb", "zb"), 0, 0, tiled=True,
    ).reshape(4, 2, 2, 2, 128, PART)
    other = to_sibling(mine)
    (sums,) = call(
        begin_kernel, [jax.ShapeDtypeStruct((2, 256, 256), full)], 2**29,
        core_at, mine, key_layer, value_layer,
    )
    give, across, grads = call(
        attend_kernel,
        [
            jax.ShapeDtypeStruct((CHIPS + 1, 256, PART), low),
            jax.ShapeDtypeStruct((128, 256), low),
            jax.ShapeDtypeStruct((2, 256, 256), low),
        ],
        2**30,
        core_at, other, sums, key_layer, value_layer, queries[0], context_grad[0],
    )
    swapped = to_sibling(give)
    got_across = to_next_chip(across)
    (keep,) = call(
        keep_kernel, [jax.ShapeDtypeStruct((CHIPS, 256, PART), full)], 2**30,
        core_at, grads, key_layer, value_layer,
    )
    (chip_sum,) = call(
        add_kernel, [jax.ShapeDtypeStruct((4, 2, 2, 2, 128, PART), low)], 2**20,
        core_at, keep, swapped,
    )
    pieces = lax.all_to_all(
        chip_sum.reshape(16, 256, PART), ("x", "yb", "zb"), 0, 0, tiled=True
    )
    piece = jnp.sum(pieces.astype(full), axis=0).astype(low).reshape(1, 2, 128, PART)
    pieces = lax.all_to_all(
        jnp.broadcast_to(piece, (2, 2, 128, PART)).reshape(4, 128, PART),
        ("z_hi", "zq"), 0, 0, tiled=True,
    )
    inside = swapped[CHIPS].reshape(2, 2, 64, PART)
    got_inside = jnp.concatenate([inside[0], inside[1]], axis=-1)
    got_across = got_across.reshape(2, 64, 256)
    passed_context = jnp.where(core == 0, got_across, got_inside)
    passed_query_grad = jnp.where(core == 0, got_inside, got_across)
    pieces, passed_context, passed_query_grad = lax.optimization_barrier(
        (pieces, passed_context, passed_query_grad)
    )
    piece = jnp.sum(pieces.astype(full), axis=0).astype(low)
    whole = lax.all_to_all(
        jnp.broadcast_to(piece[None], (8, 128, PART)), ("yq", "yb"), 0, 0, tiled=True
    )
    memory_grad = jnp.sum(whole.reshape(4, 2, 128, PART).astype(full), axis=0)
    return (passed_context[None], passed_query_grad[None], memory_grad)


def solution(mesh):
    fine = Mesh(mesh.devices.reshape(SIZES), AXES)
    section = ("zq", "zb", "x", "core")
    mp = ("z_hi", "yq", "yb")
    in_specs = (
        P(section, None, None, mp),
        P(None, None, section),
        P(section, None, mp),
        P(section, None, mp),
        P(section, None, None, mp),
    )
    out_specs = (
        P(section, None, None, mp),
        P(section, None, None, mp),
        P(None, None, section),
    )
    return jax.shard_map(
        per_device, mesh=fine, in_specs=in_specs, out_specs=out_specs, check_vma=False
    )
```

```python
import jax
import jax.numpy as jnp
from jax import lax
from jax.experimental import pallas as pl
from jax.experimental.pallas import tpu as pltpu
from jax.sharding import Mesh, PartitionSpec as P

HEAD_DIM = 256
AXES = ("zq", "zb", "x", "core", "z_hi", "yq", "yb")
SIZES = (2, 2, 4, 2, 2, 4, 2)
CHIPS = 16
PART = 128


def index_of(z_lo, x, core, z_hi, y):
    return (((z_lo * 4 + x) * 2 + core) * 2 + z_hi) * 8 + y


def routes(step):
    pairs = []
    for chip in range(CHIPS):
        for core in range(2):
            to = step(chip, core)
            if to is None:
                continue
            for z_hi in range(2):
                for y in range(8):
                    pairs.append((
                        index_of(chip // 4, chip % 4, core, z_hi, y),
                        index_of(to[0] // 4, to[0] % 4, to[1], z_hi, y),
                    ))
    return pairs


def to_sibling(block):
    return lax.ppermute(block, AXES, routes(lambda chip, core: (chip, 1 - core)))


def to_next_chip(block):
    def step(chip, core):
        chip = chip + 1 if core == 1 else chip - 1
        return (chip, 1 - core) if 0 <= chip < CHIPS else None

    return lax.ppermute(block, AXES, routes(step))


def pair(ref, block, parity):
    low = ref[pl.ds(pl.multiple_of((4 * block + parity) * PART, PART), PART), :]
    high = ref[pl.ds(pl.multiple_of((4 * block + 2 + parity) * PART, PART), PART), :]
    return jnp.concatenate([low, high], axis=0)


def dot(a, b, contract):
    return lax.dot_general(a, b, (contract, ((), ())), preferred_element_type=jnp.float32)


def block_of(features, chip):
    z_lo, x = chip // 4, chip % 4
    zb, zq = z_lo % 2, z_lo // 2
    return jnp.concatenate([features[x, 0, zb, zq], features[x, 1, zb, zq]], axis=0)


def partial_rows(features, key_ref, value_ref, parity, key_sum, value_sum):
    for block in range(CHIPS // 2):
        sides = [block_of(features, 2 * block), block_of(features, 2 * block + 1)]
        tile = jnp.concatenate(sides, axis=1)
        key_part = dot(tile, pair(key_ref, block, parity), ((1,), (0,)))
        value_part = dot(tile, pair(value_ref, block, parity), ((1,), (0,)))
        key_sum = key_part if key_sum is None else key_sum + key_part
        value_sum = value_part if value_sum is None else value_sum + value_part
    return key_sum, value_sum


def contribute(key_grad, value_grad, key_ref, value_ref, parity, block):
    part = dot(key_grad, pair(key_ref, block, parity), ((1,), (1,)))
    return part + dot(value_grad, pair(value_ref, block, parity), ((1,), (1,)))


def begin_kernel(core_ref, mine_ref, key_ref, value_ref, sum_ref):
    key_sum, value_sum = partial_rows(mine_ref, key_ref, value_ref, core_ref[0], None, None)
    sum_ref[0] = key_sum
    sum_ref[1] = value_sum


def attend_kernel(
    core_ref, other_ref, sum_ref, key_ref, value_ref, query_ref, grad_ref,
    give_ref, across_ref, grads_ref,
):
    core = core_ref[0]
    scale = HEAD_DIM ** (-0.5)
    key_sum, value_sum = partial_rows(
        other_ref, key_ref, value_ref, 1 - core, sum_ref[0], sum_ref[1]
    )
    key_rows = key_sum.astype(jnp.bfloat16)
    value_rows = value_sum.astype(jnp.bfloat16)
    contexts, query_grads = [], []
    for micro in range(2):
        keys = key_rows[micro * 128:(micro + 1) * 128]
        values = value_rows[micro * 128:(micro + 1) * 128]
        query = query_ref[micro]
        grad = grad_ref[micro]
        scores = dot(query, keys, ((1,), (1,))) * scale
        grad_probs = dot(grad, values, ((1,), (1,)))
        raised = jnp.exp(scores - jnp.max(scores, axis=-1, keepdims=True))
        attention = raised / jnp.sum(raised, axis=-1, keepdims=True)
        prob_low = attention.astype(jnp.bfloat16)
        row_dot = jnp.sum(attention * grad_probs, axis=-1, keepdims=True)
        grad_scores = (attention * (grad_probs - row_dot) * scale).astype(jnp.bfloat16)
        contexts.append(dot(prob_low, values, ((1,), (0,))).astype(jnp.bfloat16))
        query_grads.append(dot(grad_scores, keys, ((1,), (0,))).astype(jnp.bfloat16))
        rows = slice(micro * 128, (micro + 1) * 128)
        grads_ref[0, rows] = dot(grad_scores, query, ((0,), (0,))).astype(jnp.bfloat16)
        grads_ref[1, rows] = dot(prob_low, grad, ((0,), (0,))).astype(jnp.bfloat16)
    context = jnp.concatenate(contexts, axis=0)
    query_grad = jnp.concatenate(query_grads, axis=0)
    inside = jnp.where(core == 0, context, query_grad)
    across_ref[...] = jnp.where(core == 0, query_grad, context)
    give_ref[CHIPS, :128] = inside[:, :PART]
    give_ref[CHIPS, 128:] = inside[:, PART:]
    for block in range(CHIPS // 2):
        part = contribute(grads_ref[0], grads_ref[1], key_ref, value_ref, 1 - core, block)
        part = part.astype(jnp.bfloat16)
        give_ref[2 * block] = part[:, :PART]
        give_ref[2 * block + 1] = part[:, PART:]


def keep_kernel(core_ref, grads_ref, key_ref, value_ref, keep_ref):
    for block in range(CHIPS // 2):
        part = contribute(grads_ref[0], grads_ref[1], key_ref, value_ref, core_ref[0], block)
        keep_ref[2 * block] = part[:, :PART]
        keep_ref[2 * block + 1] = part[:, PART:]


def add_kernel(core_ref, keep_ref, swapped_ref, total_ref):
    for chip in range(CHIPS):
        z_lo, x = chip // 4, chip % 4
        total = keep_ref[chip] + swapped_ref[chip].astype(jnp.float32)
        total = total.astype(jnp.bfloat16)
        total_ref[x, 0, z_lo % 2, z_lo // 2] = total[:128]
        total_ref[x, 1, z_lo % 2, z_lo // 2] = total[128:]


def call(kernel, outs, flops, *args):
    specs = [pl.BlockSpec(memory_space=pltpu.SMEM)]
    specs += [pl.BlockSpec(memory_space=pltpu.VMEM)] * (len(args) - 1)
    return pl.pallas_call(
        kernel,
        out_shape=outs,
        in_specs=specs,
        out_specs=[pl.BlockSpec(memory_space=pltpu.VMEM)] * len(outs),
        compiler_params=pltpu.CompilerParams(vmem_limit_bytes=32 * 2**20),
        cost_estimate=pl.CostEstimate(flops=flops, bytes_accessed=2**22, transcendentals=0),
    )(*args)


def per_device(queries, memory, key_weight, value_weight, context_grad):
    core = lax.axis_index("core")
    core_at = core.astype(jnp.int32).reshape(1)
    key_layer, value_layer = key_weight[0], value_weight[0]
    low, full = jnp.bfloat16, jnp.float32
    half = lax.dynamic_slice_in_dim(memory, lax.axis_index("yb"), 1, 0)
    column = lax.all_to_all(jnp.broadcast_to(half, (2, 128, PART)), "zq", 0, 0, tiled=True)
    mine = lax.all_to_all(
        jnp.broadcast_to(column.reshape(1, 256, PART), (16, 256, PART)),
        ("x", "yb", "zb"), 0, 0, tiled=True,
    ).reshape(4, 2, 2, 2, 128, PART)
    other = to_sibling(mine)
    (sums,) = call(
        begin_kernel, [jax.ShapeDtypeStruct((2, 256, 256), full)], 2**29,
        core_at, mine, key_layer, value_layer,
    )
    give, across, grads = call(
        attend_kernel,
        [
            jax.ShapeDtypeStruct((CHIPS + 1, 256, PART), low),
            jax.ShapeDtypeStruct((128, 256), low),
            jax.ShapeDtypeStruct((2, 256, 256), low),
        ],
        2**30,
        core_at, other, sums, key_layer, value_layer, queries[0], context_grad[0],
    )
    swapped = to_sibling(give)
    got_across = to_next_chip(across)
    (keep,) = call(
        keep_kernel, [jax.ShapeDtypeStruct((CHIPS, 256, PART), full)], 2**30,
        core_at, grads, key_layer, value_layer,
    )
    (chip_sum,) = call(
        add_kernel, [jax.ShapeDtypeStruct((4, 2, 2, 2, 128, PART), low)], 2**20,
        core_at, keep, swapped,
    )
    pieces = lax.all_to_all(
        chip_sum.reshape(16, 256, PART), ("x", "yb", "zb"), 0, 0, tiled=True
    )
    piece = jnp.sum(pieces.astype(full), axis=0).astype(low).reshape(1, 2, 128, PART)
    pieces = lax.all_to_all(
        jnp.broadcast_to(piece, (2, 2, 128, PART)).reshape(4, 128, PART),
        ("z_hi", "zq"), 0, 0, tiled=True,
    )
    inside = swapped[CHIPS].reshape(2, 2, 64, PART)
    got_inside = jnp.concatenate([inside[0], inside[1]], axis=-1)
    got_across = got_across.reshape(2, 64, 256)
    passed_context = jnp.where(core == 0, got_across, got_inside)
    passed_query_grad = jnp.where(core == 0, got_inside, got_across)
    piece = jnp.sum(pieces.astype(full), axis=0).astype(low)
    whole = lax.all_to_all(
        jnp.broadcast_to(piece[None], (8, 128, PART)), ("yq", "yb"), 0, 0, tiled=True
    )
    memory_grad = jnp.sum(whole.reshape(4, 2, 128, PART).astype(full), axis=0)
    return (passed_context[None], passed_query_grad[None], memory_grad)


def solution(mesh):
    fine = Mesh(mesh.devices.reshape(SIZES), AXES)
    section = ("zq", "zb", "x", "core")
    mp = ("z_hi", "yq", "yb")
    in_specs = (
        P(section, None, None, mp),
        P(None, None, section),
        P(section, None, mp),
        P(section, None, mp),
        P(section, None, None, mp),
    )
    out_specs = (
        P(section, None, None, mp),
        P(section, None, None, mp),
        P(None, None, section),
    )
    return jax.shard_map(
        per_device, mesh=fine, in_specs=in_specs, out_specs=out_specs, check_vma=False
    )
```

```python
import jax
import jax.numpy as jnp
from jax import lax
from jax.experimental import pallas as pl
from jax.experimental.pallas import tpu as pltpu
from jax.sharding import Mesh, PartitionSpec as P

HEAD_DIM = 256
AXES = ("zq", "zb", "xq", "xb", "core", "z_hi", "yq", "yb")
SIZES = (2, 2, 2, 2, 2, 2, 4, 2)
CHIPS = 16
PART = 128


def index_of(z_lo, x, core, z_hi, y):
    return (((z_lo * 4 + x) * 2 + core) * 2 + z_hi) * 8 + y


def routes(step):
    pairs = []
    for chip in range(CHIPS):
        for core in range(2):
            to = step(chip, core)
            if to is None:
                continue
            for z_hi in range(2):
                for y in range(8):
                    pairs.append((
                        index_of(chip // 4, chip % 4, core, z_hi, y),
                        index_of(to[0] // 4, to[0] % 4, to[1], z_hi, y),
                    ))
    return pairs


FIRST_PAIRS = (((0, 1), (3, 2)), ((1, 2), (0, 3)))
SECOND_PAIRS = (((0, 3), (1, 2)), ((0, 1), (2, 3)))


def exchange(blocks, groups):
    return lax.all_to_all(blocks, AXES, 0, 0, tiled=True, axis_index_groups=groups)


def neighbour_groups():
    groups = []
    for core in range(2):
        for pair_x in FIRST_PAIRS[core]:
            for y in range(core, 8, 2):
                for z in range(core, 8, 2):
                    group = []
                    for member in range(8):
                        at_y, at_z = [
                            (low + (low + (member >> bit)) % 2) % 8 for low, bit in [(y, 1), (z, 0)]
                        ]
                        at_x = pair_x[member >> 2]
                        group.append(index_of(at_z % 4, at_x, core, at_z // 4, at_y))
                    groups.append(group)
    return groups


def column_groups(both_halves):
    groups = []
    for core in range(2):
        for pair_x in SECOND_PAIRS[core]:
            for y in range(8):
                for zb in range(2):
                    halves = [
                        [
                            index_of(2 * zq + zb, at_x, core, z_hi, y)
                            for zq in range(2)
                            for at_x in pair_x
                        ]
                        for z_hi in range(2)
                    ]
                    groups += [halves[0] + halves[1]] if both_halves else halves
    return groups


def to_sibling(block):
    return lax.ppermute(block, AXES, routes(lambda chip, core: (chip, 1 - core)))


def to_next_chip(block):
    def step(chip, core):
        chip = chip + 1 if core == 1 else chip - 1
        return (chip, 1 - core) if 0 <= chip < CHIPS else None

    return lax.ppermute(block, AXES, routes(step))


def pair(ref, block, parity):
    low = ref[pl.ds(pl.multiple_of((4 * block + parity) * PART, PART), PART), :]
    high = ref[pl.ds(pl.multiple_of((4 * block + 2 + parity) * PART, PART), PART), :]
    return jnp.concatenate([low, high], axis=0)


def dot(a, b, contract):
    return lax.dot_general(a, b, (contract, ((), ())), preferred_element_type=jnp.float32)


def places(chip, core):
    z_lo, x = chip // 4, chip % 4
    middle = 1 if x in (1, 2) else 0
    group = jnp.where(core == 0, middle, x // 2)
    place = jnp.where(core == 0, x // 2, x % 2)
    return group, z_lo % 2, z_lo // 2, place


def block_of(features, chip, core):
    group, zb, zq, place = places(chip, core)
    rows = [features[group, half, zb, zq, place] for half in range(2)]
    return jnp.concatenate(rows, axis=0)


def partial_rows(features, key_ref, value_ref, parity, key_sum, value_sum):
    for block in range(CHIPS // 2):
        sides = [block_of(features, 2 * block + side, parity) for side in range(2)]
        tile = jnp.concatenate(sides, axis=1)
        key_part = dot(tile, pair(key_ref, block, parity), ((1,), (0,)))
        value_part = dot(tile, pair(value_ref, block, parity), ((1,), (0,)))
        key_sum = key_part if key_sum is None else key_sum + key_part
        value_sum = value_part if value_sum is None else value_sum + value_part
    return key_sum, value_sum


def contribute(key_grad, value_grad, key_ref, value_ref, parity, block):
    part = dot(key_grad, pair(key_ref, block, parity), ((1,), (1,)))
    return part + dot(value_grad, pair(value_ref, block, parity), ((1,), (1,)))


def begin_kernel(core_ref, mine_ref, key_ref, value_ref, sum_ref):
    key_sum, value_sum = partial_rows(mine_ref, key_ref, value_ref, core_ref[0], None, None)
    sum_ref[0] = key_sum
    sum_ref[1] = value_sum


def attend_kernel(
    core_ref, other_ref, sum_ref, key_ref, value_ref, query_ref, grad_ref,
    give_ref, across_ref, grads_ref,
):
    core = core_ref[0]
    scale = HEAD_DIM ** (-0.5)
    key_sum, value_sum = partial_rows(
        other_ref, key_ref, value_ref, 1 - core, sum_ref[0], sum_ref[1]
    )
    key_rows = key_sum.astype(jnp.bfloat16)
    value_rows = value_sum.astype(jnp.bfloat16)
    micros = range(2)
    keys = [key_rows[micro * 128:(micro + 1) * 128] for micro in micros]
    values = [value_rows[micro * 128:(micro + 1) * 128] for micro in micros]
    scores = [dot(query_ref[micro], keys[micro], ((1,), (1,))) * scale for micro in micros]
    grad_probs = [dot(grad_ref[micro], values[micro], ((1,), (1,))) for micro in micros]
    scores = jnp.concatenate(scores, axis=0)
    grad_probs = jnp.concatenate(grad_probs, axis=0)
    raised = jnp.exp(scores - jnp.max(scores, axis=-1, keepdims=True))
    attention = raised / jnp.sum(raised, axis=-1, keepdims=True)
    prob_low = attention.astype(jnp.bfloat16)
    row_dot = jnp.sum(attention * grad_probs, axis=-1, keepdims=True)
    grad_scores = (attention * (grad_probs - row_dot) * scale).astype(jnp.bfloat16)
    contexts, query_grads = [], []
    for micro in micros:
        probs = prob_low[micro * 64:(micro + 1) * 64]
        slopes = grad_scores[micro * 64:(micro + 1) * 64]
        rows = slice(micro * 128, (micro + 1) * 128)
        grads_ref[1, rows] = dot(probs, grad_ref[micro], ((0,), (0,))).astype(jnp.bfloat16)
        grads_ref[0, rows] = dot(slopes, query_ref[micro], ((0,), (0,))).astype(jnp.bfloat16)
        contexts.append(dot(probs, values[micro], ((1,), (0,))).astype(jnp.bfloat16))
        query_grads.append(dot(slopes, keys[micro], ((1,), (0,))).astype(jnp.bfloat16))
    context = jnp.concatenate(contexts, axis=0)
    query_grad = jnp.concatenate(query_grads, axis=0)
    inside = jnp.where(core == 0, context, query_grad)
    across_ref[...] = jnp.where(core == 0, query_grad, context)
    give_ref[CHIPS, :128] = inside[:, :PART]
    give_ref[CHIPS, 128:] = inside[:, PART:]
    for block in range(CHIPS // 2):
        part = contribute(grads_ref[0], grads_ref[1], key_ref, value_ref, 1 - core, block)
        part = part.astype(jnp.bfloat16)
        give_ref[2 * block] = part[:, :PART]
        give_ref[2 * block + 1] = part[:, PART:]


def keep_kernel(core_ref, grads_ref, key_ref, value_ref, keep_ref):
    for block in range(CHIPS // 2):
        part = contribute(grads_ref[0], grads_ref[1], key_ref, value_ref, core_ref[0], block)
        keep_ref[2 * block] = part[:, :PART]
        keep_ref[2 * block + 1] = part[:, PART:]


def add_kernel(core_ref, keep_ref, swapped_ref, total_ref):
    for chip in range(CHIPS):
        group, zb, zq, place = places(chip, core_ref[0])
        total = keep_ref[chip] + swapped_ref[chip].astype(jnp.float32)
        total = total.astype(jnp.bfloat16)
        total_ref[group, 0, zb, zq, place] = total[:128]
        total_ref[group, 1, zb, zq, place] = total[128:]


def call(kernel, outs, flops, *args):
    specs = [pl.BlockSpec(memory_space=pltpu.SMEM)]
    specs += [pl.BlockSpec(memory_space=pltpu.VMEM)] * (len(args) - 1)
    return pl.pallas_call(
        kernel,
        out_shape=outs,
        in_specs=specs,
        out_specs=[pl.BlockSpec(memory_space=pltpu.VMEM)] * len(outs),
        compiler_params=pltpu.CompilerParams(vmem_limit_bytes=32 * 2**20),
        cost_estimate=pl.CostEstimate(flops=flops, bytes_accessed=2**22, transcendentals=0),
    )(*args)


def per_device(queries, memory, key_weight, value_weight, context_grad):
    core = lax.axis_index("core")
    core_at = core.astype(jnp.int32).reshape(1)
    key_layer, value_layer = key_weight[0], value_weight[0]
    low, full = jnp.bfloat16, jnp.float32
    half = lax.dynamic_slice_in_dim(memory, lax.axis_index("yb"), 1, 0)
    column = exchange(jnp.broadcast_to(half, (4, 128, PART)), column_groups(False))
    mine = exchange(
        jnp.broadcast_to(column.reshape(1, 512, PART), (8, 512, PART)), neighbour_groups()
    ).reshape(2, 2, 2, 2, 2, 128, PART)
    other = to_sibling(mine)
    (sums,) = call(
        begin_kernel, [jax.ShapeDtypeStruct((2, 256, 256), full)], 2**29,
        core_at, mine, key_layer, value_layer,
    )
    give, across, grads = call(
        attend_kernel,
        [
            jax.ShapeDtypeStruct((CHIPS + 1, 256, PART), low),
            jax.ShapeDtypeStruct((128, 256), low),
            jax.ShapeDtypeStruct((2, 256, 256), low),
        ],
        2**30,
        core_at, other, sums, key_layer, value_layer, queries[0], context_grad[0],
    )
    swapped = to_sibling(give)
    got_across = to_next_chip(across)
    (keep,) = call(
        keep_kernel, [jax.ShapeDtypeStruct((CHIPS, 256, PART), full)], 2**30,
        core_at, grads, key_layer, value_layer,
    )
    (chip_sum,) = call(
        add_kernel, [jax.ShapeDtypeStruct((2, 2, 2, 2, 2, 128, PART), low)], 2**20,
        core_at, keep, swapped,
    )
    pieces = exchange(chip_sum.reshape(8, 512, PART), neighbour_groups())
    piece = jnp.sum(pieces.astype(full), axis=0).astype(low).reshape(1, 4, 128, PART)
    pieces = exchange(
        jnp.broadcast_to(piece, (2, 4, 128, PART)).reshape(8, 128, PART), column_groups(True)
    )
    inside = swapped[CHIPS].reshape(2, 2, 64, PART)
    got_inside = jnp.concatenate([inside[0], inside[1]], axis=-1)
    got_across = got_across.reshape(2, 64, 256)
    passed_context = jnp.where(core == 0, got_across, got_inside)
    passed_query_grad = jnp.where(core == 0, got_inside, got_across)
    piece = jnp.sum(pieces.astype(full), axis=0).astype(low)
    whole = lax.all_to_all(
        jnp.broadcast_to(piece[None], (8, 128, PART)), ("yq", "yb"), 0, 0, tiled=True
    )
    memory_grad = jnp.sum(whole.reshape(4, 2, 128, PART).astype(full), axis=0)
    return (passed_context[None], passed_query_grad[None], memory_grad)


def solution(mesh):
    fine = Mesh(mesh.devices.reshape(SIZES), AXES)
    section = ("zq", "zb", "xq", "xb", "core")
    mp = ("z_hi", "yq", "yb")
    in_specs = (
        P(section, None, None, mp),
        P(None, None, section),
        P(section, None, mp),
        P(section, None, mp),
        P(section, None, None, mp),
    )
    out_specs = (
        P(section, None, None, mp),
        P(section, None, None, mp),
        P(None, None, section),
    )
    return jax.shard_map(
        per_device, mesh=fine, in_specs=in_specs, out_specs=out_specs, check_vma=False
    )
```

```python
import jax
import jax.numpy as jnp
from jax import lax
from jax.experimental import pallas as pl
from jax.experimental.pallas import tpu as pltpu
from jax.sharding import Mesh, PartitionSpec as P

HEAD_DIM = 256
AXES = ("zq", "zb", "xq", "xb", "core", "z_hi", "yq", "yb")
SIZES = (2, 2, 2, 2, 2, 2, 4, 2)
CHIPS = 16
PART = 128


def index_of(z_lo, x, core, z_hi, y):
    return (((z_lo * 4 + x) * 2 + core) * 2 + z_hi) * 8 + y


def routes(step):
    pairs = []
    for chip in range(CHIPS):
        for core in range(2):
            to = step(chip, core)
            if to is None:
                continue
            for z_hi in range(2):
                for y in range(8):
                    pairs.append((
                        index_of(chip // 4, chip % 4, core, z_hi, y),
                        index_of(to[0] // 4, to[0] % 4, to[1], z_hi, y),
                    ))
    return pairs


FIRST_PAIRS = (((0, 1), (3, 2)), ((1, 2), (0, 3)))
SECOND_PAIRS = (((0, 3), (1, 2)), ((0, 1), (2, 3)))


def exchange(blocks, groups):
    return lax.all_to_all(blocks, AXES, 0, 0, tiled=True, axis_index_groups=groups)


def neighbour_groups():
    groups = []
    for core in range(2):
        for pair_x in FIRST_PAIRS[core]:
            for y in range(core, 8, 2):
                for z in range(core, 8, 2):
                    group = []
                    for member in range(8):
                        at_y, at_z = [
                            (low + (low + (member >> bit)) % 2) % 8 for low, bit in [(y, 1), (z, 0)]
                        ]
                        at_x = pair_x[member >> 2]
                        group.append(index_of(at_z % 4, at_x, core, at_z // 4, at_y))
                    groups.append(group)
    return groups


def column_groups(both_halves):
    groups = []
    for core in range(2):
        for pair_x in SECOND_PAIRS[core]:
            for y in range(8):
                for zb in range(2):
                    halves = [
                        [
                            index_of(2 * zq + zb, at_x, core, z_hi, y)
                            for zq in range(2)
                            for at_x in pair_x
                        ]
                        for z_hi in range(2)
                    ]
                    groups += [halves[0] + halves[1]] if both_halves else halves
    return groups


def to_sibling(block):
    return lax.ppermute(block, AXES, routes(lambda chip, core: (chip, 1 - core)))


def to_next_chip(block):
    def step(chip, core):
        chip = chip + 1 if core == 1 else chip - 1
        return (chip, 1 - core) if 0 <= chip < CHIPS else None

    return lax.ppermute(block, AXES, routes(step))


def pair(ref, block, parity):
    low = ref[pl.ds(pl.multiple_of((4 * block + parity) * PART, PART), PART), :]
    high = ref[pl.ds(pl.multiple_of((4 * block + 2 + parity) * PART, PART), PART), :]
    return jnp.concatenate([low, high], axis=0)


def dot(a, b, contract):
    return lax.dot_general(a, b, (contract, ((), ())), preferred_element_type=jnp.float32)


def places(chip, core):
    z_lo, x = chip // 4, chip % 4
    middle = 1 if x in (1, 2) else 0
    group = jnp.where(core == 0, middle, x // 2)
    place = jnp.where(core == 0, x // 2, x % 2)
    return group, z_lo % 2, z_lo // 2, place


def block_of(features, chip, core):
    group, zb, zq, place = places(chip, core)
    rows = [features[group, half, zb, zq, place] for half in range(2)]
    return jnp.concatenate(rows, axis=0)


def partial_rows(features, key_ref, value_ref, parity, key_sum, value_sum):
    for block in range(CHIPS // 2):
        sides = [block_of(features, 2 * block + side, parity) for side in range(2)]
        tile = jnp.concatenate(sides, axis=1)
        key_part = dot(tile, pair(key_ref, block, parity), ((1,), (0,)))
        value_part = dot(tile, pair(value_ref, block, parity), ((1,), (0,)))
        key_sum = key_part if key_sum is None else key_sum + key_part
        value_sum = value_part if value_sum is None else value_sum + value_part
    return key_sum, value_sum


def contribute(key_grad, value_grad, key_ref, value_ref, parity, block):
    part = dot(key_grad, pair(key_ref, block, parity), ((1,), (1,)))
    return part + dot(value_grad, pair(value_ref, block, parity), ((1,), (1,)))


def begin_kernel(core_ref, mine_ref, key_ref, value_ref, sum_ref):
    key_sum, value_sum = partial_rows(mine_ref, key_ref, value_ref, core_ref[0], None, None)
    sum_ref[0] = key_sum
    sum_ref[1] = value_sum


def attend_kernel(
    core_ref, other_ref, sum_ref, key_ref, value_ref, query_ref, grad_ref,
    give_ref, across_ref, grads_ref,
):
    core = core_ref[0]
    scale = HEAD_DIM ** (-0.5)
    key_sum, value_sum = partial_rows(
        other_ref, key_ref, value_ref, 1 - core, sum_ref[0], sum_ref[1]
    )
    key_rows = key_sum.astype(jnp.bfloat16)
    value_rows = value_sum.astype(jnp.bfloat16)
    micros = range(2)
    keys = [key_rows[micro * 128:(micro + 1) * 128] for micro in micros]
    values = [value_rows[micro * 128:(micro + 1) * 128] for micro in micros]
    scores = [dot(query_ref[micro], keys[micro], ((1,), (1,))) * scale for micro in micros]
    grad_probs = [dot(grad_ref[micro], values[micro], ((1,), (1,))) for micro in micros]
    scores = jnp.concatenate(scores, axis=0)
    grad_probs = jnp.concatenate(grad_probs, axis=0)
    raised = jnp.exp(scores - jnp.max(scores, axis=-1, keepdims=True))
    attention = raised / jnp.sum(raised, axis=-1, keepdims=True)
    prob_low = attention.astype(jnp.bfloat16)
    row_dot = jnp.sum(attention * grad_probs, axis=-1, keepdims=True)
    grad_scores = (attention * (grad_probs - row_dot) * scale).astype(jnp.bfloat16)
    contexts, query_grads = [], []
    for micro in micros:
        probs = prob_low[micro * 64:(micro + 1) * 64]
        slopes = grad_scores[micro * 64:(micro + 1) * 64]
        rows = slice(micro * 128, (micro + 1) * 128)
        grads_ref[1, rows] = dot(probs, grad_ref[micro], ((0,), (0,))).astype(jnp.bfloat16)
        grads_ref[0, rows] = dot(slopes, query_ref[micro], ((0,), (0,))).astype(jnp.bfloat16)
        contexts.append(dot(probs, values[micro], ((1,), (0,))).astype(jnp.bfloat16))
        query_grads.append(dot(slopes, keys[micro], ((1,), (0,))).astype(jnp.bfloat16))
    context = jnp.concatenate(contexts, axis=0)
    query_grad = jnp.concatenate(query_grads, axis=0)
    inside = jnp.where(core == 0, context, query_grad)
    across_ref[...] = jnp.where(core == 0, query_grad, context)
    give_ref[CHIPS, :128] = inside[:, :PART]
    give_ref[CHIPS, 128:] = inside[:, PART:]
    for block in range(CHIPS // 2):
        part = contribute(grads_ref[0], grads_ref[1], key_ref, value_ref, 1 - core, block)
        part = part.astype(jnp.bfloat16)
        give_ref[2 * block] = part[:, :PART]
        give_ref[2 * block + 1] = part[:, PART:]


def keep_kernel(core_ref, grads_ref, key_ref, value_ref, keep_ref):
    for block in range(CHIPS // 2):
        part = contribute(grads_ref[0], grads_ref[1], key_ref, value_ref, core_ref[0], block)
        keep_ref[2 * block] = part[:, :PART]
        keep_ref[2 * block + 1] = part[:, PART:]


def add_kernel(core_ref, keep_ref, swapped_ref, total_ref):
    for chip in range(CHIPS):
        group, zb, zq, place = places(chip, core_ref[0])
        total = keep_ref[chip] + swapped_ref[chip].astype(jnp.float32)
        total = total.astype(jnp.bfloat16)
        total_ref[group, 0, zb, zq, place] = total[:128]
        total_ref[group, 1, zb, zq, place] = total[128:]


def output_kernel(
    core_ref, swapped_ref, across_ref, whole_ref, context_ref, query_ref, memory_ref
):
    core = core_ref[0]
    inside = jnp.concatenate([swapped_ref[CHIPS, :128], swapped_ref[CHIPS, 128:]], axis=1)
    across = across_ref[...]
    context = jnp.where(core == 0, across, inside)
    query_grad = jnp.where(core == 0, inside, across)
    for micro in range(2):
        rows = slice(micro * 64, (micro + 1) * 64)
        context_ref[0, micro] = context[rows]
        query_ref[0, micro] = query_grad[rows]
        total = whole_ref[micro].astype(jnp.float32)
        for pairs in range(1, 4):
            total = total + whole_ref[2 * pairs + micro].astype(jnp.float32)
        memory_ref[micro] = total


def call(kernel, outs, flops, *args):
    specs = [pl.BlockSpec(memory_space=pltpu.SMEM)]
    specs += [pl.BlockSpec(memory_space=pltpu.VMEM)] * (len(args) - 1)
    return pl.pallas_call(
        kernel,
        out_shape=outs,
        in_specs=specs,
        out_specs=[pl.BlockSpec(memory_space=pltpu.VMEM)] * len(outs),
        compiler_params=pltpu.CompilerParams(vmem_limit_bytes=32 * 2**20),
        cost_estimate=pl.CostEstimate(flops=flops, bytes_accessed=2**22, transcendentals=0),
    )(*args)


def per_device(queries, memory, key_weight, value_weight, context_grad):
    core = lax.axis_index("core")
    core_at = core.astype(jnp.int32).reshape(1)
    key_layer, value_layer = key_weight[0], value_weight[0]
    low, full = jnp.bfloat16, jnp.float32
    half = lax.dynamic_slice_in_dim(memory, lax.axis_index("yb"), 1, 0)
    column = exchange(jnp.broadcast_to(half, (4, 128, PART)), column_groups(False))
    mine = exchange(
        jnp.broadcast_to(column.reshape(1, 512, PART), (8, 512, PART)), neighbour_groups()
    ).reshape(2, 2, 2, 2, 2, 128, PART)
    other = to_sibling(mine)
    (sums,) = call(
        begin_kernel, [jax.ShapeDtypeStruct((2, 256, 256), full)], 2**29,
        core_at, mine, key_layer, value_layer,
    )
    give, across, grads = call(
        attend_kernel,
        [
            jax.ShapeDtypeStruct((CHIPS + 1, 256, PART), low),
            jax.ShapeDtypeStruct((128, 256), low),
            jax.ShapeDtypeStruct((2, 256, 256), low),
        ],
        2**30,
        core_at, other, sums, key_layer, value_layer, queries[0], context_grad[0],
    )
    swapped = to_sibling(give)
    got_across = to_next_chip(across)
    (keep,) = call(
        keep_kernel, [jax.ShapeDtypeStruct((CHIPS, 256, PART), full)], 2**30,
        core_at, grads, key_layer, value_layer,
    )
    (chip_sum,) = call(
        add_kernel, [jax.ShapeDtypeStruct((2, 2, 2, 2, 2, 128, PART), low)], 2**20,
        core_at, keep, swapped,
    )
    pieces = exchange(chip_sum.reshape(8, 512, PART), neighbour_groups())
    piece = jnp.sum(pieces.astype(full), axis=0).astype(low).reshape(1, 4, 128, PART)
    pieces = exchange(
        jnp.broadcast_to(piece, (2, 4, 128, PART)).reshape(8, 128, PART), column_groups(True)
    )
    piece = jnp.sum(pieces.astype(full), axis=0).astype(low)
    whole = lax.all_to_all(
        jnp.broadcast_to(piece[None], (8, 128, PART)), ("yq", "yb"), 0, 0, tiled=True
    )
    passed_context, passed_query_grad, memory_grad = call(
        output_kernel,
        [
            jax.ShapeDtypeStruct((1, 2, 64, 256), low),
            jax.ShapeDtypeStruct((1, 2, 64, 256), low),
            jax.ShapeDtypeStruct((2, 128, PART), full),
        ],
        2**20, core_at, swapped, got_across, whole,
    )
    return (passed_context, passed_query_grad, memory_grad)


def solution(mesh):
    fine = Mesh(mesh.devices.reshape(SIZES), AXES)
    section = ("zq", "zb", "xq", "xb", "core")
    mp = ("z_hi", "yq", "yb")
    in_specs = (
        P(section, None, None, mp),
        P(None, None, section),
        P(section, None, mp),
        P(section, None, mp),
        P(section, None, None, mp),
    )
    out_specs = (
        P(section, None, None, mp),
        P(section, None, None, mp),
        P(None, None, section),
    )
    return jax.shard_map(
        per_device, mesh=fine, in_specs=in_specs, out_specs=out_specs, check_vma=False
    )
```
